512 devices in a mesh: lsec: 8 (over x, core), rsec: 8 (over z_lo), ops: 8 (over y, z_hi).
Axes of the slice: x: 4, y: 4, z: 16 (z_hi: 2, z_lo: 8; z = z_hi * 8 + z_lo), core: 2. Of those that a mesh axis runs over, the one named last changes fastest.
Arguments:
- psi: bfloat16 [64, 64, 128, 128], P(('lsec', 'rsec')), may hold values from -6 to 6
- left_ops: bfloat16 [16, 64, 128, 128], P('ops', ('lsec', 'rsec')), may hold values from -0.5 to 0.5
- right_ops: bfloat16 [16, 64, 128, 128], P('ops', ('lsec', 'rsec')), may hold values from -0.125 to 0.125
- left_order: int32 [64], replicated, may hold values from 0 to 63, each once
- right_order: int32 [64], replicated, may hold values from 0 to 63, each once
- left_qn: int32 [64], replicated, may hold values from 0 to 2
- right_qn: int32 [64], replicated, may hold values from 0 to 2
- left_dims: int32 [64], replicated, may hold values from 96 to 128
- right_dims: int32 [64], replicated, may hold values from 96 to 128
Outputs:
- first_sigma: bfloat16 [64, 64, 128, 128], P(('lsec', 'rsec'))
- second_sigma: bfloat16 [64, 64, 128, 128], P(('lsec', 'rsec'), 'ops')
The draws below stay inside these ranges and needn't reach their ends.
Inputs may be any that keep to these rules, and one draw needn't show every extreme that they name: left_order holds each left sector once. right_order holds each right sector once.
All inputs are finite; a program needn't handle non-finite values.
Results may differ from the reference program's by a relative error of at most 0.025.
Values may be sent and summed in bfloat16 or wider, within the bound.
No kernel may reach another device: no remote copies, remote signals or barrier semaphores. Data moves between devices by JAX's collectives and lax.ppermute only.
A program may use at most 64 MiB of HBM per device.

```python
import jax
import jax.numpy as jnp
from jax import lax

M = 128
K_DEV = 2
QMAX = 3
SPREAD = 1
K = 16
NL = 64
NR = 64
N_OPS = 8


def place_ends(result, key, low, largest):
    extent = result.shape
    place = [jax.random.randint(jax.random.fold_in(key, axis), (), 0, extent[axis]) for axis in range(len(extent))]
    result = result.at[tuple(place)].set(low)
    longest = extent.index(max(extent))
    place[longest] = (place[longest] + 1) % extent[longest]
    return result.at[tuple(place)].set(largest)


def levels(stream_key, extent, shards, least, top_value):
    factor_of = 1.0
    for dim, parts in shards:
        heights = jax.random.uniform(jax.random.fold_in(jax.random.fold_in(stream_key, 6), dim), (parts,), jnp.float32, least / len(shards), top_value / len(shards))
        factor_of = factor_of * jnp.repeat(jnp.exp(heights), extent[dim] // parts).reshape((-1,) + (1,) * (len(extent) - 1 - dim))
    return factor_of


def normal_values(rng, dims, spread, bound, pieces=(), kind=jnp.bfloat16):
    entries = spread * jax.random.normal(rng, dims, jnp.float32)
    if pieces:
        entries = entries * levels(rng, dims, pieces, -0.22, 0.18)
    return jnp.clip(entries, -bound, bound).astype(kind)


def setup_inputs(seed: int = 0) -> dict:
    key_of = jax.random.split(jax.random.key(seed), 10)
    psi = normal_values(key_of[0], (NL, NR, M, M), 1.0, 6.0, ((0, 64),))
    left_ops = normal_values(key_of[1], (K, NL, M, M), M ** -0.5, 0.5, ((0, 8), (1, 64)))
    right_ops = normal_values(key_of[2], (K, NR, M, M), (M * K) ** -0.5, 0.125, ((0, 8), (1, 64)))
    left_order = jax.random.permutation(key_of[3], NL).astype(jnp.int32)
    right_order = jax.random.permutation(key_of[4], NR).astype(jnp.int32)
    left_qn = place_ends(jax.random.randint(key_of[5], (NL,), 0, QMAX), jax.random.fold_in(key_of[5], 1), 0, QMAX - 1).astype(jnp.int32)
    right_qn = place_ends(jax.random.randint(key_of[6], (NR,), 0, QMAX), jax.random.fold_in(key_of[6], 1), 0, QMAX - 1).astype(jnp.int32)
    left_dims = place_ends(jax.random.randint(key_of[7], (NL,), 3 * M // 4, M + 1), jax.random.fold_in(key_of[7], 1), 3 * M // 4, M).astype(jnp.int32)
    right_dims = place_ends(jax.random.randint(key_of[8], (NR,), 3 * M // 4, M + 1), jax.random.fold_in(key_of[8], 1), 3 * M // 4, M).astype(jnp.int32)
    return {"psi": psi, "left_ops": left_ops, "right_ops": right_ops, "left_order": left_order, "right_order": right_order, "left_qn": left_qn, "right_qn": right_qn, "left_dims": left_dims, "right_dims": right_dims}


def projector(left_qn, right_qn, left_dims, right_dims):
    allowed = jnp.abs(left_qn[:, None] - right_qn[None, :]) <= SPREAD
    line = jnp.arange(M, dtype=jnp.int32)
    rows = line[None, :] < left_dims[:, None]
    cols = line[None, :] < right_dims[:, None]
    return allowed[:, :, None, None] & rows[:, None, :, None] & cols[None, :, None, :]


def inverse(order, count):
    return jnp.zeros((count,), jnp.int32).at[order].set(jnp.arange(count, dtype=jnp.int32))


def apply_terms(state, left_id, right_id, left_first):
    values = state.astype(jnp.float32)

    def group(total, group_index):
        def term(acc, inner_index):
            k = group_index * K_DEV + inner_index
            left_block = left_id[k].astype(jnp.float32)
            right_block = right_id[k].astype(jnp.float32)
            if left_first:
                inner = jnp.einsum("axy,abyz->abxz", left_block, values).astype(jnp.bfloat16)
                inner = lax.optimization_barrier(inner).astype(jnp.float32)
                outer = jnp.einsum("abxy,bzy->abxz", inner, right_block)
            else:
                inner = jnp.einsum("abxy,bzy->abxz", values, right_block).astype(jnp.bfloat16)
                inner = lax.optimization_barrier(inner).astype(jnp.float32)
                outer = jnp.einsum("axy,abyz->abxz", left_block, inner)
            return acc + outer, None

        part, _ = lax.scan(term, jnp.zeros(values.shape, jnp.float32), jnp.arange(K_DEV, dtype=jnp.int32))
        part = lax.optimization_barrier(part.astype(jnp.bfloat16)).astype(jnp.float32)
        return total + part, None

    summed, _ = lax.scan(group, jnp.zeros(values.shape, jnp.float32), jnp.arange(N_OPS, dtype=jnp.int32))
    return summed


def reference(psi, left_ops, right_ops, left_order, right_order, left_qn, right_qn, left_dims, right_dims):
    inv_left = inverse(left_order, NL)
    inv_right = inverse(right_order, NR)
    mask = projector(left_qn, right_qn, left_dims, right_dims)
    left_id = left_ops[:, inv_left]
    right_id = right_ops[:, inv_right]
    start = jnp.where(mask, psi[inv_left], jnp.zeros((), jnp.bfloat16))
    first_id = jnp.where(mask, apply_terms(start, left_id, right_id, True), 0.0).astype(jnp.bfloat16)
    second_id = jnp.where(mask, apply_terms(first_id, left_id, right_id, False), 0.0).astype(jnp.bfloat16)
    first_sigma = jnp.transpose(first_id[:, right_order], (1, 0, 2, 3))
    second_sigma = second_id[left_order]
    return first_sigma, second_sigma
```

```python
import jax
import jax.numpy as jnp
import numpy as np
from jax import lax
from jax.sharding import Mesh
from jax.sharding import PartitionSpec as P

SPREAD = 1
NX, NC, NZ, NY, NH = 4, 2, 8, 4, 2
AXES = ("x", "c", "z", "y", "h")
SLOT = ("x", "c", "z")
SHIFT = np.array(
    [
        [[0, 4], [0, -4]],
        [[1, -3], [-1, 3]],
        [[-1, 3], [1, -3]],
        [[2, -2], [-2, 2]],
    ],
    np.int32,
)
HOLDER_Y = np.zeros((NC, NZ), np.int32)
HOLDER_N = np.zeros((NC, NZ), np.int32)
for _y in range(NY):
    for _c in range(NC):
        for _n in range(2):
            HOLDER_Y[_c, SHIFT[_y, _c, _n] % NZ] = _y
            HOLDER_N[_c, SHIFT[_y, _c, _n] % NZ] = _n


def index_of(x, c, z, y):
    return (((x * NC + c) * NZ + z % NZ) * NY + y) * NH + (z // NZ) % NH


def moved(target):
    pairs = []
    for x in range(NX):
        for c in range(NC):
            for z in range(NZ * NH):
                for y in range(NY):
                    pairs.append((index_of(x, c, z, y), index_of(*target(x, c, z % 16, y))))
    return pairs


def permute(value, target):
    return lax.ppermute(value, AXES, moved(lambda x, c, z, y: target(x, c, z, y)))


def shift_z(value, n, sign):
    return permute(
        value, lambda x, c, z, y: (x, c, (z + sign * int(SHIFT[y, c, n])) % 16, y)
    )


def swap_half(value):
    return permute(value, lambda x, c, z, y: (x, c, (z + 8) % 16, y))


def swap_core(value):
    return permute(value, lambda x, c, z, y: (x, 1 - c, z, y))


def inverse(order):
    count = order.shape[0]
    return jnp.zeros((count,), jnp.int32).at[order].set(jnp.arange(count, dtype=jnp.int32))


def on_device(
    psi, left_ops, right_ops, left_order, right_order, left_qn, right_qn, left_dims, right_dims
):
    x, c, z = lax.axis_index("x"), lax.axis_index("c"), lax.axis_index("z")
    y, h = lax.axis_index("y"), lax.axis_index("h")
    slot = (x * NC + c) * NZ + z
    m = psi.shape[-1]
    line = jnp.arange(m, dtype=jnp.int32)
    zero = jnp.zeros((), jnp.bfloat16)
    inv_left = inverse(left_order)
    inv_right = inverse(right_order)
    shift = jnp.asarray(SHIFT)
    holder_y = jnp.asarray(HOLDER_Y)
    holder_n = jnp.asarray(HOLDER_N)

    def mask(a, b):
        allowed = jnp.abs(left_qn[a] - right_qn[b]) <= SPREAD
        rows = line < left_dims[a][..., None]
        cols = line < right_dims[b][..., None]
        return allowed[..., None, None] & rows[..., :, None] & cols[..., None, :]

    with jax.named_scope("half_exchange"):
        own = jnp.concatenate([left_ops[:, 0], right_ops[:, 0]], 0)
        other = swap_half(own)
    low = jnp.where(h == 0, own, other)
    high = jnp.where(h == 0, other, own)
    left4 = jnp.concatenate([low[:2], high[:2]], 0)
    right4 = jnp.concatenate([low[2:], high[2:]], 0)
    with jax.named_scope("left_terms_over_y"):
        left16 = lax.all_to_all(
            jnp.broadcast_to(left4[None], (NY,) + left4.shape), "y", 0, 0, tiled=True
        ).reshape(16, m, m)
    with jax.named_scope("left_shift"):
        left_own = jnp.stack([shift_z(left16, n, -1) for n in range(2)])
    with jax.named_scope("right_over_xy"):
        right = lax.all_to_all(
            jnp.broadcast_to(right4[None], (NX * NY,) + right4.shape), ("x", "y"), 0, 0, tiled=True
        ).reshape(NX, 16, m, m)
    with jax.named_scope("left_core"):
        left = jnp.stack([left_own, swap_core(left_own)])

    here = left_order[slot]
    plane = jnp.arange(NX * NC, dtype=jnp.int32) * NZ
    with jax.named_scope("psi_shift"):
        moved_psi = []
        for n in range(2):
            target = (z - shift[y, c, n]) % NZ
            b = right_order[plane + target]
            block = jnp.where(mask(here, b), psi[0][b], zero)
            moved_psi.append(shift_z(block, n, -1))
        got = jnp.stack(moved_psi).reshape(2, NX, NC, m, m)
    with jax.named_scope("psi_core"):
        keep = jnp.where(c == 0, got[:, :, 0], got[:, :, 1])
        give = jnp.where(c == 0, got[:, :, 1], got[:, :, 0])
        start = jnp.stack([keep, swap_core(give)])

    core = jnp.stack([c, 1 - c])
    left_slot = (x * NC + core[:, None]) * NZ + (z + shift[y][core]) % NZ
    a4 = left_order[left_slot]
    b4 = right_order[(jnp.arange(NX) * NC + c) * NZ + z]
    mask16 = mask(a4[:, :, None], b4[None, None, :])

    with jax.named_scope("first"):
        inner = jnp.einsum(
            "cnkpq,cnxqr->cnxpkr", left, start, preferred_element_type=jnp.float32
        ).astype(jnp.bfloat16)
        first = jnp.einsum("cnxpkr,xksr->xcnps", inner, right, preferred_element_type=jnp.float32)
        first = jnp.where(jnp.moveaxis(mask16, 2, 0), first, 0.0).astype(jnp.bfloat16)
    with jax.named_scope("first_out"):
        sent = jnp.broadcast_to(first[:, None], (NX, NY) + first.shape[1:])
        came = lax.all_to_all(
            sent.reshape((NX * NY,) + first.shape[1:]), ("x", "y"), 0, 0, tiled=True
        ).reshape(64, m, m)
        from_slot = inv_left
        from_x, from_c, from_z = from_slot // (NC * NZ), (from_slot // NZ) % NC, from_slot % NZ
        delta = (from_z - z) % NZ
        place = (
            (from_x * NY + holder_y[from_c, delta]) * 4
            + jnp.where(from_c == c, 0, 2)
            + holder_n[from_c, delta]
        )
        first_out = came[place]

    with jax.named_scope("second"):
        inner = jnp.einsum(
            "xcnpq,xkrq->xcnkpr", first, right, preferred_element_type=jnp.float32
        ).astype(jnp.bfloat16)
        second = jnp.einsum(
            "cnkpq,xcnkqr->cnxpr", left, inner, preferred_element_type=jnp.float32
        ).astype(jnp.bfloat16)
    with jax.named_scope("second_core"):
        theirs = swap_core(second[1])
        both = jnp.where(
            c == 0, jnp.stack([second[0], theirs], 2), jnp.stack([theirs, second[0]], 2)
        ).reshape(2, NX * NC, m, m)
    with jax.named_scope("second_shift"):
        back = jnp.concatenate([shift_z(both[n], n, 1) for n in range(2)], 0)
    with jax.named_scope("second_over_y"):
        b_all = (
            (jnp.arange(NY, dtype=jnp.int32)[:, None] * NH + h) * 8
            + jnp.arange(8, dtype=jnp.int32)[None, :]
        )
        j = inv_right[b_all]
        j_xc, j_z = j // NZ, j % NZ
        delta = (z - j_z) % NZ
        owner = holder_y[c, delta]
        position = holder_n[c, delta] * (NX * NC) + j_xc
        packed = back[position.reshape(-1)]
        arrived = lax.all_to_all(packed, "y", 0, 0, tiled=True).reshape(NY, 8, m, m)
        chosen = arrived[owner[y], jnp.arange(8)]
        b8 = b_all[y]
        second_out = jnp.where(mask(here, b8), chosen, zero)
    return first_out[None], second_out[None]


def solution(mesh):
    fine = Mesh(mesh.devices.reshape(NX, NC, NZ, NY, NH), AXES)
    slots, ops = P(SLOT), P(("y", "h"), SLOT)
    return jax.shard_map(
        on_device,
        mesh=fine,
        in_specs=(slots, ops, ops, P(), P(), P(), P(), P(), P()),
        out_specs=(slots, P(SLOT, ("y", "h"))),
        check_vma=False,
    )
```

```python
import jax
import jax.numpy as jnp
import numpy as np
from jax import lax
from jax.experimental import pallas as pl
from jax.experimental.pallas import tpu as pltpu
from jax.sharding import Mesh
from jax.sharding import PartitionSpec as P

SPREAD = 1
M = 128
NX, NC, NZ, NY, NH = 4, 2, 8, 4, 2
NK = 16
AXES = ("x", "c", "z", "y", "h")
SLOT = ("x", "c", "z")
SHIFT = np.array(
    [
        [[0, 4], [0, -4]],
        [[1, -3], [-1, 3]],
        [[-1, 3], [1, -3]],
        [[2, -2], [-2, 2]],
    ],
    np.int32,
)
HOLDER_Y = np.zeros((NC, NZ), np.int32)
for _y in range(NY):
    for _c in range(NC):
        for _n in range(2):
            HOLDER_Y[_c, SHIFT[_y, _c, _n] % NZ] = _y
LEFT_ORDER, RIGHT_ORDER, LEFT_QN, RIGHT_QN, LEFT_DIMS, RIGHT_DIMS, SHIFTS, HOLDERS = range(8)
CONSTANT_ROWS = np.zeros((2, 64), np.int32)
CONSTANT_ROWS[0, : SHIFT.size] = SHIFT.reshape(-1)
CONSTANT_ROWS[1, : HOLDER_Y.size] = HOLDER_Y.reshape(-1)


def index_of(x, c, z, y):
    return (((x * NC + c) * NZ + z % NZ) * NY + y) * NH + (z // NZ) % NH


def permute(value, target):
    pairs = []
    for x in range(NX):
        for c in range(NC):
            for z in range(NZ * NH):
                for y in range(NY):
                    to_c, to_z = target(c, z, y)
                    pairs.append((index_of(x, c, z, y), index_of(x, to_c, to_z % 16, y)))
    return lax.ppermute(value, AXES, pairs)


def here():
    return tuple(lax.axis_index(name) for name in AXES)


def shift_of(tab, y, c, n):
    return tab[SHIFTS, (y * NC + c) * 2 + n]


def slot_of(x, c, z):
    return (x * NC + c) * NZ + lax.rem(z + 2 * NZ, NZ)


def limits(tab, a, b):
    allowed = jnp.abs(tab[LEFT_QN, a] - tab[RIGHT_QN, b]) <= SPREAD
    return jnp.where(allowed, tab[LEFT_DIMS, a], 0), tab[RIGHT_DIMS, b]


def masked(block, tab, a, b):
    rows, cols = limits(tab, a, b)
    row = lax.broadcasted_iota(jnp.int32, (M, M), 0)
    col = lax.broadcasted_iota(jnp.int32, (M, M), 1)
    return jnp.where((row < rows) & (col < cols), block.astype(jnp.float32), 0.0)


def psi_kernel(tab, psi, keep0, keep1, give0, give1, sems):
    x, c, z, y, h = here()
    a = tab[LEFT_ORDER, slot_of(x, c, z)]
    work = []
    for n, (keep, give) in enumerate(((keep0, give0), (keep1, give1))):
        to_z = z - shift_of(tab, y, c, n)
        for out, to_c in ((keep, c), (give, 1 - c)):
            for to_x in range(NX):
                b = tab[RIGHT_ORDER, slot_of(to_x, to_c, to_z)]
                copy = pltpu.make_async_copy(psi.at[b], out.at[to_x], sems.at[len(work)])
                copy.start()
                work.append((copy, out, to_x, b))
    for copy, out, to_x, b in work:
        copy.wait()
        out[to_x] = masked(out[to_x], tab, a, b).astype(jnp.bfloat16)


def products_kernel(
    tab, lo0, lo1, lx0, lx1, right, so0, so1, sx0, sx1,
    send, keep0, keep1, give0, give1,
    left_v, right_v, state_v, inner_v, sems_l, sems_r, sems_s, sems_o,
):
    x, c, z, y, h = here()
    state_copies, right_copies, left_copies = [], [], []
    for i, source in enumerate((so0, so1, sx0, sx1)):
        copy = pltpu.make_async_copy(source, state_v.at[:, i], sems_s.at[i])
        copy.start()
        state_copies.append(copy)
    for j in range(NX):
        copy = pltpu.make_async_copy(right.at[j], right_v.at[j], sems_r.at[j])
        copy.start()
        right_copies.append(copy)
    for i, source in enumerate((lo0, lo1, lx0, lx1)):
        for k in range(NK):
            copy = pltpu.make_async_copy(
                source.at[k], left_v.at[i, :, pl.ds(k * M, M)], sems_l.at[i, k]
            )
            copy.start()
            left_copies.append(copy)

    def product(ready):
        for j in range(NX):
            if ready is not None:
                ready[j].wait()
            state = state_v[j].reshape(4 * M, M)
            for pair in range(NK // 2):
                term = right_v[j, 2 * pair : 2 * pair + 2].reshape(2 * M, M)
                inner = lax.dot_general(
                    state, term, (((1,), (1,)), ((), ())), preferred_element_type=jnp.float32
                ).astype(jnp.bfloat16)
                for i in range(4):
                    for half in range(2):
                        k = 2 * pair + half
                        inner_v[i, k * M : (k + 1) * M, j * M : (j + 1) * M] = inner[
                            i * M : (i + 1) * M, half * M : (half + 1) * M
                        ]

    def total(i):
        return jnp.dot(left_v[i], inner_v[i], preferred_element_type=jnp.float32)

    for copy in state_copies:
        copy.wait()
    product(right_copies)
    for copy in left_copies:
        copy.wait()
    for i in range(4):
        value = total(i)
        core = c if i < 2 else 1 - c
        a = tab[LEFT_ORDER, slot_of(x, core, z + shift_of(tab, y, core, i % 2))]
        for j in range(NX):
            b = tab[RIGHT_ORDER, slot_of(j, c, z)]
            state_v[j, i] = masked(value[:, j * M : (j + 1) * M], tab, a, b).astype(jnp.bfloat16)
    out_copies = []
    for j in range(NX):
        for to_y in range(NY):
            copy = pltpu.make_async_copy(
                state_v.at[j], send.at[j, to_y], sems_o.at[j, to_y]
            )
            copy.start()
            out_copies.append(copy)
    product(None)
    for i, out in enumerate((keep0, keep1, give0, give1)):
        value = total(i).astype(jnp.bfloat16)
        for j in range(NX):
            out[j] = value[:, j * M : (j + 1) * M]
    for copy in out_copies:
        copy.wait()


def first_kernel(tab, came, out, sem):
    x, c, z, y, h = here()
    copies = []
    for from_x in range(NX):
        for from_y in range(NY):
            for i in range(4):
                core = c if i < 2 else 1 - c
                slot = slot_of(from_x, core, z + shift_of(tab, from_y, core, i % 2))
                a = tab[LEFT_ORDER, slot]
                place = (from_x * NY + from_y) * 4 + i
                copy = pltpu.make_async_copy(came.at[place], out.at[a], sem.at[place])
                copy.start()
                copies.append(copy)
    for copy in copies:
        copy.wait()


def pack_kernel(tab, keep0, keep1, give0, give1, out, sems):
    x, c, z, y, h = here()
    work = []
    for n, (keep, give) in enumerate(((keep0, give0), (keep1, give1))):
        from_z = z - shift_of(tab, y, c, n)
        for source, from_c in ((keep, c), (give, 1 - c)):
            for from_x in range(NX):
                b = tab[RIGHT_ORDER, slot_of(from_x, from_c, from_z)]
                group = b // 8
                wanted = lax.rem(group, NH) == h
                copy = pltpu.make_async_copy(
                    source.at[from_x], out.at[group // NH, lax.rem(b, 8)], sems.at[len(work)]
                )
                work.append((wanted, copy))
    for wanted, copy in work:
        pl.when(wanted)(copy.start)
    for wanted, copy in work:
        pl.when(wanted)(copy.wait)


def second_kernel(tab, arrived, out, sems):
    x, c, z, y, h = here()
    a = tab[LEFT_ORDER, slot_of(x, c, z)]
    mine = y * NH + h

    def visit(slot, carry):
        b = tab[RIGHT_ORDER, slot]
        from_y = tab[HOLDERS, c * NZ + lax.rem(z - lax.rem(slot, NZ) + NZ, NZ)]
        q = lax.rem(b, 8)

        @pl.when(b // 8 == mine)
        def _():
            pltpu.make_async_copy(arrived.at[from_y, q], out.at[q], sems.at[q]).start()

        return carry

    lax.fori_loop(0, 64, visit, 0)
    for q in range(8):
        pltpu.make_async_copy(arrived.at[0, q], out.at[q], sems.at[q]).wait()
        out[q] = masked(out[q], tab, a, mine * 8 + q).astype(jnp.bfloat16)


ANY = pl.BlockSpec(memory_space=pl.ANY)
VMEM = pl.BlockSpec(memory_space=pltpu.VMEM)
SMEM = pl.BlockSpec(memory_space=pltpu.SMEM)
DMA = pltpu.SemaphoreType.DMA


def blocks(*shape):
    return jax.ShapeDtypeStruct(shape + (M, M), jnp.bfloat16)


def call(kernel, name, inputs, out_shape, out_specs, scratch, flops=0, size=0, vmem=32 << 20):
    return pl.pallas_call(
        kernel,
        name=name,
        out_shape=out_shape,
        in_specs=[SMEM] + [ANY] * (len(inputs) - 1),
        out_specs=out_specs,
        scratch_shapes=scratch,
        cost_estimate=pl.CostEstimate(flops=flops, bytes_accessed=size, transcendentals=0),
        compiler_params=pltpu.CompilerParams(vmem_limit_bytes=vmem),
    )(*inputs)


def on_device(
    psi, left_ops, right_ops, left_order, right_order, left_qn, right_qn, left_dims, right_dims
):
    h = lax.axis_index("h")
    tab = jnp.concatenate(
        [
            jnp.stack([left_order, right_order, left_qn, right_qn, left_dims, right_dims]),
            jnp.asarray(CONSTANT_ROWS),
        ]
    )

    with jax.named_scope("half_exchange"):
        left_own, right_own = left_ops[:, 0], right_ops[:, 0]
        left_other = permute(left_own, lambda c, z, y: (c, z + 8))
        right_other = permute(right_own, lambda c, z, y: (c, z + 8))

    def both(own, other):
        return jnp.where(
            h == 0, jnp.concatenate([own, other], 0), jnp.concatenate([other, own], 0)
        )

    with jax.named_scope("psi_shift"):
        packed = call(
            psi_kernel, "psi_pack", (tab, psi[0]), [blocks(NX)] * 4, [VMEM] * 4, [DMA((16,))],
            size=1 << 20,
        )
        starts = []
        for part in range(2):
            for n in range(2):
                starts.append(
                    permute(
                        packed[2 * part + n],
                        lambda c, z, y: (c ^ part, z - int(SHIFT[y, c, n])),
                    )
                )

    with jax.named_scope("left_over_y"):
        left4 = both(left_own, left_other)
        left16 = lax.all_to_all(
            jnp.broadcast_to(left4[None], (NY,) + left4.shape), "y", 0, 0, tiled=True
        ).reshape(NK, M, M)
    with jax.named_scope("left_shift"):
        left_kept = [
            permute(left16, lambda c, z, y: (c, z - int(SHIFT[y, c, n]))) for n in range(2)
        ]
    with jax.named_scope("left_core"):
        left_got = [permute(value, lambda c, z, y: (1 - c, z)) for value in left_kept]
    with jax.named_scope("right_over_xy"):
        right4 = both(right_own, right_other)
        right4, left16 = lax.optimization_barrier((right4, left16))
        right = lax.all_to_all(
            jnp.broadcast_to(right4[None], (NX * NY,) + right4.shape), ("x", "y"), 0, 0, tiled=True
        ).reshape(NX, NK, M, M)

    with jax.named_scope("products"):
        sent, *seconds = call(
            products_kernel,
            "products",
            (tab, *left_kept, *left_got, right, *starts),
            [blocks(NX, NY, 4)] + [blocks(NX)] * 4,
            [ANY] + [VMEM] * 4,
            [
                pltpu.VMEM((4, M, NK * M), jnp.bfloat16),
                pltpu.VMEM((NX, NK, M, M), jnp.bfloat16),
                pltpu.VMEM((NX, 4, M, M), jnp.bfloat16),
                pltpu.VMEM((4, NK * M, NX * M), jnp.bfloat16),
                DMA((4, NK)), DMA((NX,)), DMA((4,)), DMA((NX, NY)),
            ],
            flops=2 * 2 * 16 * NK * 2 * M**3,
            size=8 << 20,
            vmem=48 << 20,
        )
    with jax.named_scope("first_out"):
        came = lax.all_to_all(
            sent.reshape(NX * NY, 4, M, M), ("x", "y"), 0, 0, tiled=True
        ).reshape(64, M, M)
    with jax.named_scope("second_shift"):
        back = []
        for part in range(2):
            for n in range(2):
                back.append(
                    permute(
                        seconds[2 * part + n],
                        lambda c, z, y: (c ^ part, z + int(SHIFT[y, c ^ part, n])),
                    )
                )
    with jax.named_scope("second_over_y"):
        gathered = call(
            pack_kernel, "second_pack", (tab, *back), blocks(NY, 8), ANY, [DMA((16,))],
            size=1 << 20,
        )
        gathered, came = lax.optimization_barrier((gathered, came))
        arrived = lax.all_to_all(gathered, "y", 0, 0, tiled=True)
    with jax.named_scope("first_order"):
        first_out = call(
            first_kernel, "first_order", (tab, came), blocks(64), ANY, [DMA((64,))], size=4 << 20
        )
    with jax.named_scope("second_pick"):
        second_out = call(
            second_kernel, "second_pick", (tab, arrived), blocks(8), VMEM, [DMA((8,))],
            size=1 << 19,
        )
    return first_out[None], second_out[None]


def solution(mesh):
    fine = Mesh(mesh.devices.reshape(NX, NC, NZ, NY, NH), AXES)
    slots, ops = P(SLOT), P(("y", "h"), SLOT)
    return jax.shard_map(
        on_device,
        mesh=fine,
        in_specs=(slots, ops, ops, P(), P(), P(), P(), P(), P()),
        out_specs=(slots, P(SLOT, ("y", "h"))),
        check_vma=False,
    )
```

```python
import functools

import jax
import jax.numpy as jnp
import numpy as np
from jax import lax
from jax.experimental import pallas as pl
from jax.experimental.pallas import tpu as pltpu
from jax.sharding import Mesh
from jax.sharding import PartitionSpec as P

SPREAD = 1
PSI_FIRST = True
OUT_FIRST = True
M = 128
NX, NC, NZ, NY, NH = 4, 2, 8, 4, 2
NK = 16
AXES = ("x", "c", "z", "y", "h")
SLOT = ("x", "c", "z")
SHIFT = np.array(
    [
        [[0, 4], [0, -4]],
        [[1, -3], [-1, 3]],
        [[-1, 3], [1, -3]],
        [[2, -2], [-2, 2]],
    ],
    np.int32,
)
HOLDER_Y = np.zeros((NC, NZ), np.int32)
for _y in range(NY):
    for _c in range(NC):
        for _n in range(2):
            HOLDER_Y[_c, SHIFT[_y, _c, _n] % NZ] = _y
LEFT_ORDER, RIGHT_ORDER, LEFT_QN, RIGHT_QN, LEFT_DIMS, RIGHT_DIMS, SHIFTS, HOLDERS = range(8)
CONSTANT_ROWS = np.zeros((2, 64), np.int32)
CONSTANT_ROWS[0, : SHIFT.size] = SHIFT.reshape(-1)
CONSTANT_ROWS[1, : HOLDER_Y.size] = HOLDER_Y.reshape(-1)


def index_of(x, c, z, y):
    return (((x * NC + c) * NZ + z % NZ) * NY + y) * NH + (z // NZ) % NH


def permute(value, target):
    pairs = []
    for x in range(NX):
        for c in range(NC):
            for z in range(NZ * NH):
                for y in range(NY):
                    pairs.append((index_of(x, c, z, y), index_of(*target(x, c, z, y))))
    return lax.ppermute(value, AXES, pairs)


def from_half(value):
    return permute(value, lambda x, c, z, y: (x, c, z + 8, y))


def from_core(value):
    return permute(value, lambda x, c, z, y: (x, 1 - c, z, y))


def from_x(value, r):
    return permute(value, lambda x, c, z, y: ((x - r) % NX, c, z, y))


def from_y(value, r):
    return permute(value, lambda x, c, z, y: (x, c, z, (y - r) % NY))


def from_shift(value, n):
    return permute(value, lambda x, c, z, y: (x, c, z - int(SHIFT[y, c, n]), y))


def to_shift(value, n):
    return permute(value, lambda x, c, z, y: (x, c, z + int(SHIFT[y, c, n]), y))


def here():
    return tuple(lax.axis_index(name) for name in AXES)


def shift_of(tab, y, c, n):
    return tab[SHIFTS, (y * NC + c) * 2 + n]


def slot_of(x, c, z):
    return (x * NC + c) * NZ + lax.rem(z + 2 * NZ, NZ)


def limits(tab, a, b):
    allowed = jnp.abs(tab[LEFT_QN, a] - tab[RIGHT_QN, b]) <= SPREAD
    return jnp.where(allowed, tab[LEFT_DIMS, a], 0), tab[RIGHT_DIMS, b]


def masked(block, tab, a, b):
    rows, cols = limits(tab, a, b)
    row = lax.broadcasted_iota(jnp.int32, (M, M), 0)
    col = lax.broadcasted_iota(jnp.int32, (M, M), 1)
    return jnp.where((row < rows) & (col < cols), block.astype(jnp.float32), 0.0)


def right_sector(tab, x, c, z, j):
    return tab[RIGHT_ORDER, slot_of(lax.rem(x + j % NX, NX), c if j < NX else 1 - c, z)]


def terms_kernel(*refs):
    x, c, z, y, h = here()
    left, right = refs[-2:]
    for r in range(NY):
        for half in range(2):
            source = refs[2 * r + half]
            place = lax.rem(y + r, NY) * 4 + 2 * (h if half == 0 else 1 - h)
            for k in range(2):
                left[place + k] = source[k]
                right[place + k] = source[2 + k]


def sent_kernel(keep, got, out):
    x = lax.axis_index("x")
    for r in range(NX):
        to_x = lax.rem(x + r, NX)
        for to_y in range(NY):
            for n in range(2):
                out[to_x * NY + to_y, n] = keep[r, n]
                out[to_x * NY + to_y, 2 + n] = got[r, n]


def psi_kernel(tab, psi, out0, out1):
    x, c, z, y, h = here()
    a = tab[LEFT_ORDER, slot_of(x, c, z)]
    for n, out in enumerate((out0, out1)):
        to_z = z - shift_of(tab, y, c, n)
        for j in range(2 * NX):
            b = right_sector(tab, x, c, to_z, j)
            out[j] = masked(psi[b], tab, a, b).astype(jnp.bfloat16)


def product(state_of, left, right, inner):
    for j in range(2 * NX):
        for group in range(NK // 4):
            terms = right[j][4 * group : 4 * group + 4].reshape(4 * M, M)
            value = lax.dot_general(
                state_of(j), terms, (((1,), (1,)), ((), ())), preferred_element_type=jnp.float32
            ).astype(jnp.bfloat16)
            for n in range(2):
                for part in range(4):
                    k = 4 * group + part
                    inner[n, k * M : (k + 1) * M, j * M : (j + 1) * M] = value[
                        n * M : (n + 1) * M, part * M : (part + 1) * M
                    ]
    for n in range(2):
        row = jnp.concatenate([left[n][k] for k in range(NK)], axis=1)
        yield jnp.dot(row, inner[n], preferred_element_type=jnp.float32)


def first_product_kernel(tab, *refs):
    left, right, starts, (keep, give, inner) = refs[:2], refs[2:10], refs[10:12], refs[12:]
    x, c, z, y, h = here()

    def state_of(j):
        return jnp.concatenate([starts[0][j], starts[1][j]], axis=0)

    for n, value in enumerate(product(state_of, left, right, inner)):
        a = tab[LEFT_ORDER, slot_of(x, c, z + shift_of(tab, y, c, n))]
        for j in range(2 * NX):
            b = right_sector(tab, x, c, z, j)
            block = masked(value[:, j * M : (j + 1) * M], tab, a, b).astype(jnp.bfloat16)
            (keep if j < NX else give)[j % NX, n] = block


def second_product_kernel(*refs):
    left, right, (keep, give, out0, out1, inner) = refs[:2], refs[2:10], refs[10:]

    def state_of(j):
        return (keep if j < NX else give)[j % NX].reshape(2 * M, M)

    for out, value in zip((out0, out1), product(state_of, left, right, inner)):
        for j in range(2 * NX):
            out[j] = value[:, j * M : (j + 1) * M].astype(jnp.bfloat16)


def first_order_kernel(tab, came, out):
    x, c, z, y, h = here()
    for x_from in range(NX):
        for y_from in range(NY):
            for i in range(4):
                core = c if i < 2 else 1 - c
                slot = slot_of(x_from, core, z + shift_of(tab, y_from, core, i % 2))
                out[tab[LEFT_ORDER, slot]] = came[(x_from * NY + y_from) * 4 + i]


def second_pack_kernel(tab, back0, back1, out0, out1, out2, out3, packed):
    x, c, z, y, h = here()
    packed[...] = jnp.zeros(packed.shape, packed.dtype)
    for n, back in enumerate((back0, back1)):
        z_from = z - shift_of(tab, y, c, n)
        for j in range(2 * NX):
            b = right_sector(tab, x, c, z_from, j)
            group = b // 8

            @pl.when(lax.rem(group, NH) == h)
            def _(j=j, b=b, back=back, group=group):
                packed[lax.rem(group // NH - y + NY, NY), lax.rem(b, 8)] = back[j]

    for r, out in enumerate((out0, out1, out2, out3)):
        out[...] = packed[r]


def second_pick_kernel(tab, part0, part1, part2, part3, out):
    x, c, z, y, h = here()
    a = tab[LEFT_ORDER, slot_of(x, c, z)]
    for q in range(8):
        value = part0[q].astype(jnp.float32)
        for part in (part1, part2, part3):
            value = value + part[q].astype(jnp.float32)
        out[q] = masked(value, tab, a, (y * NH + h) * 8 + q).astype(jnp.bfloat16)


VMEM = pl.BlockSpec(memory_space=pltpu.VMEM)
SMEM = pl.BlockSpec(memory_space=pltpu.SMEM)


def blocks(*shape):
    return jax.ShapeDtypeStruct(shape + (M, M), jnp.bfloat16)


def call(kernel, name, inputs, outputs, scratch=(), flops=0, size=0, vmem=16 << 20):
    return pl.pallas_call(
        kernel,
        name=name,
        out_shape=outputs,
        in_specs=[SMEM if v.dtype == jnp.int32 else VMEM for v in inputs],
        out_specs=jax.tree.map(lambda _: VMEM, outputs),
        scratch_shapes=list(scratch),
        cost_estimate=pl.CostEstimate(flops=flops, bytes_accessed=size, transcendentals=0),
        compiler_params=pltpu.CompilerParams(vmem_limit_bytes=vmem),
    )(*inputs)


def on_device(
    psi, left_ops, right_ops, left_order, right_order, left_qn, right_qn, left_dims, right_dims
):
    h = lax.axis_index("h")
    with jax.named_scope("half_exchange"):
        own = jnp.concatenate([left_ops[:, 0], right_ops[:, 0]], 0)
        other = from_half(own)
    with jax.named_scope("own_over_y"):
        pieces = [[own]] + [[from_y(own, r)] for r in range(1, NY)]
    with jax.named_scope("psi_pack"):
        tab = jnp.concatenate(
            [
                jnp.stack([left_order, right_order, left_qn, right_qn, left_dims, right_dims]),
                jnp.asarray(CONSTANT_ROWS),
            ]
        )
        packed = call(psi_kernel, "psi_pack", (tab, psi[0]), [blocks(8)] * 2, size=3 << 20)
        other, *packed = lax.optimization_barrier((other, *packed))
    with jax.named_scope("other_over_y"):
        pieces[0].append(other)
        for r in range(1, NY):
            pieces[r].append(from_y(other, r))
    with jax.named_scope("psi_shift"):
        starts = [from_shift(packed[n], n) for n in range(2)]
    with jax.named_scope("terms"):
        if PSI_FIRST:
            pieces, starts = lax.optimization_barrier((pieces, starts))
        left16, right16 = call(
            terms_kernel, "terms", sum(pieces, []), [blocks(NK)] * 2, size=2 << 20
        )
    with jax.named_scope("left_shift"):
        left = [from_shift(left16, n) for n in range(2)]
    with jax.named_scope("right_over_x"):
        right = [right16] + [from_x(right16, r) for r in range(1, NX)]
    with jax.named_scope("right_core"):
        right = right + [from_core(value) for value in right]

    inner = [pltpu.VMEM((2, NK * M, 8 * M), jnp.bfloat16)]
    flops = 2 * 16 * NK * 2 * M**3
    with jax.named_scope("first_product"):
        keep, give = call(
            first_product_kernel, "first_product", (tab, *left, *right, *starts),
            [blocks(NX, 2)] * 2, inner, flops, 6 << 20, 32 << 20,
        )
    with jax.named_scope("first_core"):
        got = from_core(give)
    with jax.named_scope("second_product"):
        seconds = call(
            second_product_kernel, "second_product", (*left, *right, keep, give),
            [blocks(8)] * 2, inner, flops, 6 << 20, 32 << 20,
        )
    with jax.named_scope("first_out"):
        got, *seconds = lax.optimization_barrier((got, *seconds))
        sent = call(sent_kernel, "first_sent", (keep, got), blocks(NX * NY, 4), size=2 << 20)
        came = lax.all_to_all(sent, ("x", "y"), 0, 0, tiled=True).reshape(64, M, M)
    with jax.named_scope("second_shift"):
        back = [to_shift(seconds[n], n) for n in range(2)]
    with jax.named_scope("second_over_y"):
        parts = call(
            second_pack_kernel, "second_pack", (tab, *back), [blocks(8)] * NY,
            [pltpu.VMEM((NY, 8, M, M), jnp.bfloat16)], size=2 << 20,
        )
        if OUT_FIRST:
            came, *parts = lax.optimization_barrier((came, *parts))
        parts = [parts[0]] + [from_y(parts[r], -r) for r in range(1, NY)]
    with jax.named_scope("first_order"):
        first_out = call(first_order_kernel, "first_order", (tab, came), blocks(64), size=4 << 20)
    with jax.named_scope("second_pick"):
        second_out = call(
            second_pick_kernel, "second_pick", (tab, *parts), blocks(8), size=2 << 20
        )
    return first_out[None], second_out[None]


def solution(mesh):
    fine = Mesh(mesh.devices.reshape(NX, NC, NZ, NY, NH), AXES)
    slots, ops = P(SLOT), P(("y", "h"), SLOT)
    return jax.shard_map(
        on_device,
        mesh=fine,
        in_specs=(slots, ops, ops, P(), P(), P(), P(), P(), P()),
        out_specs=(slots, P(SLOT, ("y", "h"))),
        check_vma=False,
    )
```

```python
import functools

import jax
import jax.numpy as jnp
import numpy as np
from jax import lax
from jax.experimental import pallas as pl
from jax.experimental.pallas import tpu as pltpu
from jax.sharding import Mesh
from jax.sharding import PartitionSpec as P

SPREAD = 1
M = 128
NX, NC, NZ, NY, NH = 4, 2, 8, 4, 2
NK = 16
AXES = ("x", "c", "z", "y", "h")
SLOT = ("x", "c", "z")
SHIFT = np.array(
    [
        [[4, 0], [-4, 0]],
        [[-3, 1], [3, -1]],
        [[3, -1], [-3, 1]],
        [[2, -2], [-2, 2]],
    ],
    np.int32,
)
HOLDER_Y = np.zeros((NC, NZ), np.int32)
for _y in range(NY):
    for _c in range(NC):
        for _n in range(2):
            HOLDER_Y[_c, SHIFT[_y, _c, _n] % NZ] = _y
LEFT_ORDER, RIGHT_ORDER, LEFT_QN, RIGHT_QN, LEFT_DIMS, RIGHT_DIMS, SHIFTS, HOLDERS = range(8)
CONSTANT_ROWS = np.zeros((2, 64), np.int32)
CONSTANT_ROWS[0, : SHIFT.size] = SHIFT.reshape(-1)
CONSTANT_ROWS[1, : HOLDER_Y.size] = HOLDER_Y.reshape(-1)


def index_of(x, c, z, y):
    return (((x * NC + c) * NZ + z % NZ) * NY + y) * NH + (z // NZ) % NH


def permute(value, target):
    pairs = []
    for x in range(NX):
        for c in range(NC):
            for z in range(NZ * NH):
                for y in range(NY):
                    pairs.append((index_of(x, c, z, y), index_of(*target(x, c, z, y))))
    return lax.ppermute(value, AXES, pairs)


def from_half(value):
    return permute(value, lambda x, c, z, y: (x, c, z + 8, y))


def from_core(value):
    return permute(value, lambda x, c, z, y: (x, 1 - c, z, y))


def from_x(value, r):
    return permute(value, lambda x, c, z, y: ((x - r) % NX, c, z, y))


def from_y(value, r):
    return permute(value, lambda x, c, z, y: (x, c, z, (y - r) % NY))


def from_shift(value, n):
    return permute(value, lambda x, c, z, y: (x, c, z - int(SHIFT[y, c, n]), y))


def to_shift(value, n):
    return permute(value, lambda x, c, z, y: (x, c, z + int(SHIFT[y, c, n]), y))


def here():
    return tuple(lax.axis_index(name) for name in AXES)


def shift_of(tab, y, c, n):
    return tab[SHIFTS, (y * NC + c) * 2 + n]


def slot_of(x, c, z):
    return (x * NC + c) * NZ + lax.rem(z + 2 * NZ, NZ)


def limits(tab, a, b):
    allowed = jnp.abs(tab[LEFT_QN, a] - tab[RIGHT_QN, b]) <= SPREAD
    return jnp.where(allowed, tab[LEFT_DIMS, a], 0), tab[RIGHT_DIMS, b]


def masked(block, tab, a, b):
    rows, cols = limits(tab, a, b)
    row = lax.broadcasted_iota(jnp.int32, (M, M), 0)
    col = lax.broadcasted_iota(jnp.int32, (M, M), 1)
    return jnp.where((row < rows) & (col < cols), block.astype(jnp.float32), 0.0)


def right_sector(tab, x, c, z, j):
    return tab[RIGHT_ORDER, slot_of(lax.rem(x + j % NX, NX), c if j < NX else 1 - c, z)]


def terms_kernel(*refs):
    x, c, z, y, h = here()
    left, right = refs[-2:]
    for r in range(NY):
        for half in range(2):
            place = lax.rem(y + r, NY) * 4 + 2 * (h if half == 0 else 1 - h)
            for k in range(2):
                left[place + k] = refs[r][4 * half + k]
                right[place + k] = refs[r][4 * half + 2 + k]


def sent_kernel(keep, got, out):
    x = lax.axis_index("x")
    for r in range(NX):
        to_x = lax.rem(x + r, NX)
        for to_y in range(NY):
            for n in range(2):
                out[to_x * NY + to_y, n] = keep[r, n]
                out[to_x * NY + to_y, 2 + n] = got[r, n]


def psi_kernel(tab, psi, out0, out1):
    x, c, z, y, h = here()
    a = tab[LEFT_ORDER, slot_of(x, c, z)]
    for n, out in enumerate((out0, out1)):
        to_z = z - shift_of(tab, y, c, n)
        for j in range(2 * NX):
            b = right_sector(tab, x, c, to_z, j)
            out[j] = masked(psi[b], tab, a, b).astype(jnp.bfloat16)


def product(state_of, left, right, inner):
    for j in range(2 * NX):
        for group in range(NK // 4):
            terms = right[j][4 * group : 4 * group + 4].reshape(4 * M, M)
            value = lax.dot_general(
                state_of(j), terms, (((1,), (1,)), ((), ())), preferred_element_type=jnp.float32
            ).astype(jnp.bfloat16)
            for n in range(2):
                for part in range(4):
                    k = 4 * group + part
                    inner[n, k * M : (k + 1) * M, j * M : (j + 1) * M] = value[
                        n * M : (n + 1) * M, part * M : (part + 1) * M
                    ]
    for n in range(2):
        row = jnp.concatenate([left[n][k] for k in range(NK)], axis=1)
        yield jnp.dot(row, inner[n], preferred_element_type=jnp.float32)


def first_product_kernel(tab, *refs):
    left, right, starts, (keep, give, inner) = refs[:2], refs[2:10], refs[10:12], refs[12:]
    x, c, z, y, h = here()

    def state_of(j):
        return jnp.concatenate([starts[0][j], starts[1][j]], axis=0)

    for n, value in enumerate(product(state_of, left, right, inner)):
        a = tab[LEFT_ORDER, slot_of(x, c, z + shift_of(tab, y, c, n))]
        for j in range(2 * NX):
            b = right_sector(tab, x, c, z, j)
            block = masked(value[:, j * M : (j + 1) * M], tab, a, b).astype(jnp.bfloat16)
            (keep if j < NX else give)[j % NX, n] = block


def second_product_kernel(*refs):
    left, right, (keep, give, out0, out1, inner) = refs[:2], refs[2:10], refs[10:]

    def state_of(j):
        return (keep if j < NX else give)[j % NX].reshape(2 * M, M)

    for out, value in zip((out0, out1), product(state_of, left, right, inner)):
        for j in range(2 * NX):
            out[j] = value[:, j * M : (j + 1) * M].astype(jnp.bfloat16)


def first_order_kernel(tab, came, out):
    x, c, z, y, h = here()
    for x_from in range(NX):
        for y_from in range(NY):
            for i in range(4):
                core = c if i < 2 else 1 - c
                slot = slot_of(x_from, core, z + shift_of(tab, y_from, core, i % 2))
                out[tab[LEFT_ORDER, slot]] = came[(x_from * NY + y_from) * 4 + i]


def second_pack_kernel(tab, back0, back1, out0, out1, out2, out3, packed):
    x, c, z, y, h = here()
    packed[...] = jnp.zeros(packed.shape, packed.dtype)
    for n, back in enumerate((back0, back1)):
        z_from = z - shift_of(tab, y, c, n)
        for j in range(2 * NX):
            b = right_sector(tab, x, c, z_from, j)
            group = b // 8

            @pl.when(lax.rem(group, NH) == h)
            def _(j=j, b=b, back=back, group=group):
                packed[lax.rem(group // NH - y + NY, NY), lax.rem(b, 8)] = back[j]

    for r, out in enumerate((out0, out1, out2, out3)):
        out[...] = packed[r]


def second_pick_kernel(tab, part0, part1, part2, part3, out):
    x, c, z, y, h = here()
    a = tab[LEFT_ORDER, slot_of(x, c, z)]
    for q in range(8):
        value = part0[q].astype(jnp.float32)
        for part in (part1, part2, part3):
            value = value + part[q].astype(jnp.float32)
        out[q] = masked(value, tab, a, (y * NH + h) * 8 + q).astype(jnp.bfloat16)


VMEM = pl.BlockSpec(memory_space=pltpu.VMEM)
SMEM = pl.BlockSpec(memory_space=pltpu.SMEM)


def blocks(*shape):
    return jax.ShapeDtypeStruct(shape + (M, M), jnp.bfloat16)


def call(kernel, name, inputs, outputs, scratch=(), flops=0, size=0, vmem=8 << 20):
    return pl.pallas_call(
        kernel,
        name=name,
        out_shape=outputs,
        in_specs=[SMEM if v.dtype == jnp.int32 else VMEM for v in inputs],
        out_specs=jax.tree.map(lambda _: VMEM, outputs),
        scratch_shapes=list(scratch),
        cost_estimate=pl.CostEstimate(flops=flops, bytes_accessed=size, transcendentals=0),
        compiler_params=pltpu.CompilerParams(vmem_limit_bytes=vmem),
    )(*inputs)


def on_device(
    psi, left_ops, right_ops, left_order, right_order, left_qn, right_qn, left_dims, right_dims
):
    h = lax.axis_index("h")
    with jax.named_scope("half_exchange"):
        own = jnp.concatenate([left_ops[:, 0], right_ops[:, 0]], 0)
        other = from_half(own)
    with jax.named_scope("psi_pack"):
        tab = jnp.concatenate(
            [
                jnp.stack([left_order, right_order, left_qn, right_qn, left_dims, right_dims]),
                jnp.asarray(CONSTANT_ROWS),
            ]
        )
        packed = call(psi_kernel, "psi_pack", (tab, psi[0]), [blocks(8)] * 2, size=3 << 20)
    with jax.named_scope("over_y"):
        pieces = [jnp.concatenate([own, other], 0)]
        pieces += [from_y(pieces[0], r) for r in range(1, NY)]
    with jax.named_scope("psi_shift"):
        starts = [from_shift(packed[n], n) for n in range(2)]
    with jax.named_scope("terms"):
        pieces, starts = lax.optimization_barrier((pieces, starts))
        left16, right16 = call(
            terms_kernel, "terms", pieces, [blocks(NK)] * 2, size=2 << 20
        )
    with jax.named_scope("right_core"):
        right_swapped = from_core(right16)
    with jax.named_scope("left_shift"):
        left = [from_shift(left16, n) for n in range(2)]
    with jax.named_scope("right_over_x"):
        right = [right16] + [from_x(right16, r) for r in range(1, NX)]
    with jax.named_scope("right_core"):
        right = right + [right_swapped] + [from_core(value) for value in right[1:]]

    inner = [pltpu.VMEM((2, NK * M, 8 * M), jnp.bfloat16)]
    flops = 2 * 16 * NK * 2 * M**3
    with jax.named_scope("first_product"):
        keep, give = call(
            first_product_kernel, "first_product", (tab, *left, *right, *starts),
            [blocks(NX, 2)] * 2, inner, flops, 6 << 20, 20 << 20,
        )
    with jax.named_scope("first_core"):
        got = from_core(give)
    with jax.named_scope("second_product"):
        seconds = call(
            second_product_kernel, "second_product", (*left, *right, keep, give),
            [blocks(8)] * 2, inner, flops, 6 << 20, 20 << 20,
        )
    with jax.named_scope("second_shift"):
        back = [to_shift(seconds[n], n) for n in range(2)]
    with jax.named_scope("first_out"):
        got, *seconds = lax.optimization_barrier((got, *seconds))
        sent = call(sent_kernel, "first_sent", (keep, got), blocks(NX * NY, 4), size=2 << 20)
        came = lax.all_to_all(sent, ("x", "y"), 0, 0, tiled=True).reshape(64, M, M)
    with jax.named_scope("second_over_y"):
        parts = call(
            second_pack_kernel, "second_pack", (tab, *back), [blocks(8)] * NY,
            [pltpu.VMEM((NY, 8, M, M), jnp.bfloat16)], size=2 << 20,
        )
        parts = [parts[0]] + [from_y(parts[r], -r) for r in range(1, NY)]
    with jax.named_scope("first_order"):
        first_out = call(first_order_kernel, "first_order", (tab, came), blocks(64), size=4 << 20)
    first_out, *parts = lax.optimization_barrier((first_out, *parts))
    with jax.named_scope("second_pick"):
        second_out = call(
            second_pick_kernel, "second_pick", (tab, *parts), blocks(8), size=2 << 20
        )
    return first_out[None], second_out[None]


def solution(mesh):
    fine = Mesh(mesh.devices.reshape(NX, NC, NZ, NY, NH), AXES)
    slots, ops = P(SLOT), P(("y", "h"), SLOT)
    return jax.shard_map(
        on_device,
        mesh=fine,
        in_specs=(slots, ops, ops, P(), P(), P(), P(), P(), P()),
        out_specs=(slots, P(SLOT, ("y", "h"))),
        check_vma=False,
    )
```

```python
import functools

import jax
import jax.numpy as jnp
import numpy as np
from jax import lax
from jax.experimental import pallas as pl
from jax.experimental.pallas import tpu as pltpu
from jax.sharding import Mesh
from jax.sharding import PartitionSpec as P

SPREAD = 1
M = 128
NX, NC, NZ, NY, NH = 4, 2, 8, 4, 2
NK = 16
AXES = ("x", "c", "z", "y", "h")
SLOT = ("x", "c", "z")
SHIFT = np.array(
    [
        [[0, 4], [0, -4]],
        [[1, -3], [-1, 3]],
        [[-1, 3], [1, -3]],
        [[2, -2], [-2, 2]],
    ],
    np.int32,
)
HOLDER_Y = np.zeros((NC, NZ), np.int32)
for _y in range(NY):
    for _c in range(NC):
        for _n in range(2):
            HOLDER_Y[_c, SHIFT[_y, _c, _n] % NZ] = _y
LEFT_ORDER, RIGHT_ORDER, LEFT_QN, RIGHT_QN, LEFT_DIMS, RIGHT_DIMS, SHIFTS, HOLDERS = range(8)
CONSTANT_ROWS = np.zeros((2, 64), np.int32)
CONSTANT_ROWS[0, : SHIFT.size] = SHIFT.reshape(-1)
CONSTANT_ROWS[1, : HOLDER_Y.size] = HOLDER_Y.reshape(-1)


def index_of(x, c, z, y):
    return (((x * NC + c) * NZ + z % NZ) * NY + y) * NH + (z // NZ) % NH


def permute(value, target):
    pairs = []
    for x in range(NX):
        for c in range(NC):
            for z in range(NZ * NH):
                for y in range(NY):
                    pairs.append((index_of(x, c, z, y), index_of(*target(x, c, z, y))))
    return lax.ppermute(value, AXES, pairs)


def from_half(value):
    return permute(value, lambda x, c, z, y: (x, c, z + 8, y))


def from_core(value):
    return permute(value, lambda x, c, z, y: (x, 1 - c, z, y))


def from_x(value, r):
    return permute(value, lambda x, c, z, y: ((x - r) % NX, c, z, y))


def from_y(value, r):
    return permute(value, lambda x, c, z, y: (x, c, z, (y - r) % NY))


def from_shift(value, n):
    return permute(value, lambda x, c, z, y: (x, c, z - int(SHIFT[y, c, n]), y))


def to_shift(value, n):
    return permute(value, lambda x, c, z, y: (x, c, z + int(SHIFT[y, c, n]), y))


def here():
    return tuple(lax.axis_index(name) for name in AXES)


def shift_of(tab, y, c, n):
    return tab[SHIFTS, (y * NC + c) * 2 + n]


def slot_of(x, c, z):
    return (x * NC + c) * NZ + lax.rem(z + 2 * NZ, NZ)


def limits(tab, a, b):
    allowed = jnp.abs(tab[LEFT_QN, a] - tab[RIGHT_QN, b]) <= SPREAD
    return jnp.where(allowed, tab[LEFT_DIMS, a], 0), tab[RIGHT_DIMS, b]


def masked(block, tab, a, b):
    rows, cols = limits(tab, a, b)
    row = lax.broadcasted_iota(jnp.int32, (M, M), 0)
    col = lax.broadcasted_iota(jnp.int32, (M, M), 1)
    return jnp.where((row < rows) & (col < cols), block.astype(jnp.float32), 0.0)


def right_sector(tab, x, c, z, j):
    return tab[RIGHT_ORDER, slot_of(lax.rem(x + j % NX, NX), c if j < NX else 1 - c, z)]


def terms_kernel(*refs):
    x, c, z, y, h = here()
    left, right = refs[-2:]
    for r in range(NY):
        for half in range(2):
            place = lax.rem(y + r, NY) * 4 + 2 * (h if half == 0 else 1 - h)
            for k in range(2):
                left[place + k] = refs[r][4 * half + k]
                right[place + k] = refs[r][4 * half + 2 + k]


def psi_kernel(tab, psi, out0, out1):
    x, c, z, y, h = here()
    a = tab[LEFT_ORDER, slot_of(x, c, z)]
    for n, out in enumerate((out0, out1)):
        to_z = z - shift_of(tab, y, c, n)
        for j in range(2 * NX):
            b = right_sector(tab, x, c, to_z, j)
            out[j] = masked(psi[b], tab, a, b).astype(jnp.bfloat16)


def product(state_of, left, right, inner):
    for j in range(2 * NX):
        for group in range(NK // 4):
            terms = right[j][4 * group : 4 * group + 4].reshape(4 * M, M)
            value = lax.dot_general(
                state_of(j), terms, (((1,), (1,)), ((), ())), preferred_element_type=jnp.float32
            ).astype(jnp.bfloat16)
            for n in range(2):
                for part in range(4):
                    k = 4 * group + part
                    inner[n, k * M : (k + 1) * M, j * M : (j + 1) * M] = value[
                        n * M : (n + 1) * M, part * M : (part + 1) * M
                    ]
    for n in range(2):
        row = jnp.concatenate([left[n][k] for k in range(NK)], axis=1)
        yield jnp.dot(row, inner[n], preferred_element_type=jnp.float32)


def products_kernel(tab, *refs):
    left, right, starts = refs[:2], refs[2:10], refs[10:12]
    sent, out0, out1, first, inner = refs[12:]
    x, c, z, y, h = here()

    def states(j):
        return jnp.concatenate([starts[0][j], starts[1][j]], axis=0)

    for n, value in enumerate(product(states, left, right, inner)):
        a = tab[LEFT_ORDER, slot_of(x, c, z + shift_of(tab, y, c, n))]
        for j in range(2 * NX):
            b = right_sector(tab, x, c, z, j)
            block = masked(value[:, j * M : (j + 1) * M], tab, a, b).astype(jnp.bfloat16)
            first[j, n] = block
            to_x, to_c = lax.rem(x + j % NX, NX), c if j < NX else 1 - c
            for to_y in range(NY):
                sent[(to_x * NC + to_c) * NY + to_y, n] = block

    def second_states(j):
        return first[j].reshape(2 * M, M)

    for out, value in zip((out0, out1), product(second_states, left, right, inner)):
        for j in range(2 * NX):
            out[j] = value[:, j * M : (j + 1) * M].astype(jnp.bfloat16)


def first_order_kernel(tab, came, out):
    x, c, z, y, h = here()
    for x_from in range(NX):
        for c_from in range(NC):
            for y_from in range(NY):
                for n in range(2):
                    slot = slot_of(x_from, c_from, z + shift_of(tab, y_from, c_from, n))
                    place = ((x_from * NC + c_from) * NY + y_from) * 2 + n
                    out[tab[LEFT_ORDER, slot]] = came[place]


def second_pack_kernel(tab, back0, back1, out0, out1, out2, out3, packed):
    x, c, z, y, h = here()
    packed[...] = jnp.zeros(packed.shape, packed.dtype)
    for n, back in enumerate((back0, back1)):
        z_from = z - shift_of(tab, y, c, n)
        for j in range(2 * NX):
            b = right_sector(tab, x, c, z_from, j)
            group = b // 8

            @pl.when(lax.rem(group, NH) == h)
            def _(j=j, b=b, back=back, group=group):
                packed[lax.rem(group // NH - y + NY, NY), lax.rem(b, 8)] = back[j]

    for r, out in enumerate((out0, out1, out2, out3)):
        out[...] = packed[r]


def second_pick_kernel(tab, part0, part1, part2, part3, out):
    x, c, z, y, h = here()
    a = tab[LEFT_ORDER, slot_of(x, c, z)]
    for q in range(8):
        value = part0[q].astype(jnp.float32)
        for part in (part1, part2, part3):
            value = value + part[q].astype(jnp.float32)
        out[q] = masked(value, tab, a, (y * NH + h) * 8 + q).astype(jnp.bfloat16)


VMEM = pl.BlockSpec(memory_space=pltpu.VMEM)
SMEM = pl.BlockSpec(memory_space=pltpu.SMEM)


def blocks(*shape):
    return jax.ShapeDtypeStruct(shape + (M, M), jnp.bfloat16)


def call(kernel, name, inputs, outputs, scratch=(), flops=0, size=0, vmem=8 << 20):
    return pl.pallas_call(
        kernel,
        name=name,
        out_shape=outputs,
        in_specs=[SMEM if v.dtype == jnp.int32 else VMEM for v in inputs],
        out_specs=jax.tree.map(lambda _: VMEM, outputs),
        scratch_shapes=list(scratch),
        cost_estimate=pl.CostEstimate(flops=flops, bytes_accessed=size, transcendentals=0),
        compiler_params=pltpu.CompilerParams(vmem_limit_bytes=vmem),
    )(*inputs)


def on_device(
    psi, left_ops, right_ops, left_order, right_order, left_qn, right_qn, left_dims, right_dims
):
    h = lax.axis_index("h")
    with jax.named_scope("half_exchange"):
        own = jnp.concatenate([left_ops[:, 0], right_ops[:, 0]], 0)
        other = from_half(own)
    with jax.named_scope("psi_pack"):
        tab = jnp.concatenate(
            [
                jnp.stack([left_order, right_order, left_qn, right_qn, left_dims, right_dims]),
                jnp.asarray(CONSTANT_ROWS),
            ]
        )
        packed = call(psi_kernel, "psi_pack", (tab, psi[0]), [blocks(8)] * 2, size=3 << 20)
    with jax.named_scope("over_y"):
        pieces = [jnp.concatenate([own, other], 0)]
        pieces += [from_y(pieces[0], r) for r in range(1, NY)]
    with jax.named_scope("psi_shift"):
        starts = [from_shift(packed[n], n) for n in range(2)]
    with jax.named_scope("terms"):
        pieces, starts = lax.optimization_barrier((pieces, starts))
        left16, right16 = call(
            terms_kernel, "terms", pieces, [blocks(NK)] * 2, size=2 << 20
        )
    with jax.named_scope("right_core"):
        right_swapped = from_core(right16)
    with jax.named_scope("left_shift"):
        left = [from_shift(left16, n) for n in range(2)]
    with jax.named_scope("right_over_x"):
        right = [right16] + [from_x(right16, r) for r in range(1, NX)]
    with jax.named_scope("right_core"):
        right = right + [right_swapped] + [from_core(value) for value in right[1:]]

    with jax.named_scope("products"):
        sent, *seconds = call(
            products_kernel, "products", (tab, *left, *right, *starts),
            [blocks(NX * NC * NY, 2), blocks(8), blocks(8)],
            [
                pltpu.VMEM((2 * NX, 2, M, M), jnp.bfloat16),
                pltpu.VMEM((2, NK * M, 8 * M), jnp.bfloat16),
            ],
            4 * 16 * NK * 2 * M**3, 8 << 20, 20 << 20,
        )
    with jax.named_scope("first_out"):
        came = lax.all_to_all(sent, ("x", "c", "y"), 0, 0, tiled=True).reshape(64, M, M)
    with jax.named_scope("second_shift"):
        back = [to_shift(seconds[n], n) for n in range(2)]
    with jax.named_scope("second_over_y"):
        parts = call(
            second_pack_kernel, "second_pack", (tab, *back), [blocks(8)] * NY,
            [pltpu.VMEM((NY, 8, M, M), jnp.bfloat16)], size=2 << 20,
        )
        parts = [parts[0]] + [from_y(parts[r], -r) for r in range(1, NY)]
    with jax.named_scope("first_order"):
        first_out = call(first_order_kernel, "first_order", (tab, came), blocks(64), size=4 << 20)
    first_out, *parts = lax.optimization_barrier((first_out, *parts))
    with jax.named_scope("second_pick"):
        second_out = call(
            second_pick_kernel, "second_pick", (tab, *parts), blocks(8), size=2 << 20
        )
    return first_out[None], second_out[None]


def solution(mesh):
    fine = Mesh(mesh.devices.reshape(NX, NC, NZ, NY, NH), AXES)
    slots, ops = P(SLOT), P(("y", "h"), SLOT)
    return jax.shard_map(
        on_device,
        mesh=fine,
        in_specs=(slots, ops, ops, P(), P(), P(), P(), P(), P()),
        out_specs=(slots, P(SLOT, ("y", "h"))),
        check_vma=False,
    )
```

```python
import functools

import jax
import jax.numpy as jnp
import numpy as np
from jax import lax
from jax.experimental import pallas as pl
from jax.experimental.pallas import tpu as pltpu
from jax.sharding import Mesh
from jax.sharding import PartitionSpec as P

SPREAD = 1
M = 128
NX, NC, NZ, NY, NH = 4, 2, 8, 4, 2
NK = 16
AXES = ("x", "c", "z", "y", "h")
SLOT = ("x", "c", "z")
SHIFT = np.array(
    [
        [[0, 4], [0, -4]],
        [[1, -3], [-1, 3]],
        [[-1, 3], [1, -3]],
        [[2, -2], [-2, 2]],
    ],
    np.int32,
)
HOLDER_Y = np.zeros((NC, NZ), np.int32)
for _y in range(NY):
    for _c in range(NC):
        for _n in range(2):
            HOLDER_Y[_c, SHIFT[_y, _c, _n] % NZ] = _y
LEFT_ORDER, RIGHT_ORDER, LEFT_QN, RIGHT_QN, LEFT_DIMS, RIGHT_DIMS, SHIFTS, HOLDERS = range(8)
CONSTANT_ROWS = np.zeros((2, 64), np.int32)
CONSTANT_ROWS[0, : SHIFT.size] = SHIFT.reshape(-1)
CONSTANT_ROWS[1, : HOLDER_Y.size] = HOLDER_Y.reshape(-1)


def index_of(x, c, z, y):
    return (((x * NC + c) * NZ + z % NZ) * NY + y) * NH + (z // NZ) % NH


def permute(value, target):
    pairs = []
    for x in range(NX):
        for c in range(NC):
            for z in range(NZ * NH):
                for y in range(NY):
                    pairs.append((index_of(x, c, z, y), index_of(*target(x, c, z, y))))
    return lax.ppermute(value, AXES, pairs)


def from_half(value):
    return permute(value, lambda x, c, z, y: (x, c, z + 8, y))


def from_core(value):
    return permute(value, lambda x, c, z, y: (x, 1 - c, z, y))


def from_x(value, r):
    return permute(value, lambda x, c, z, y: ((x - r) % NX, c, z, y))


def from_y(value, r):
    return permute(value, lambda x, c, z, y: (x, c, z, (y - r) % NY))


def from_shift(value, n):
    return permute(value, lambda x, c, z, y: (x, c, z - int(SHIFT[y, c, n]), y))


def to_shift(value, n):
    return permute(value, lambda x, c, z, y: (x, c, z + int(SHIFT[y, c, n]), y))


def here():
    return tuple(lax.axis_index(name) for name in AXES)


def shift_of(tab, y, c, n):
    return tab[SHIFTS, (y * NC + c) * 2 + n]


def slot_of(x, c, z):
    return (x * NC + c) * NZ + lax.rem(z + 2 * NZ, NZ)


def limits(tab, a, b):
    allowed = jnp.abs(tab[LEFT_QN, a] - tab[RIGHT_QN, b]) <= SPREAD
    return jnp.where(allowed, tab[LEFT_DIMS, a], 0), tab[RIGHT_DIMS, b]


def masked(block, tab, a, b):
    rows, cols = limits(tab, a, b)
    row = lax.broadcasted_iota(jnp.int32, (M, M), 0)
    col = lax.broadcasted_iota(jnp.int32, (M, M), 1)
    return jnp.where((row < rows) & (col < cols), block.astype(jnp.float32), 0.0)


def right_sector(tab, x, c, z, j):
    return tab[RIGHT_ORDER, slot_of(lax.rem(x + j % NX, NX), c if j < NX else 1 - c, z)]


def terms_kernel(*refs):
    x, c, z, y, h = here()
    left, right = refs[-2:]
    for r in range(NY):
        for half in range(2):
            place = lax.rem(y + r, NY) * 4 + 2 * (h if half == 0 else 1 - h)
            for k in range(2):
                left[place + k] = refs[r][4 * half + k]
                right[place + k] = refs[r][4 * half + 2 + k]


def psi_kernel(tab, psi, out0, out1):
    x, c, z, y, h = here()
    a = tab[LEFT_ORDER, slot_of(x, c, z)]
    for n, out in enumerate((out0, out1)):
        to_z = z - shift_of(tab, y, c, n)
        for j in range(2 * NX):
            b = right_sector(tab, x, c, to_z, j)
            out[j] = masked(psi[b], tab, a, b).astype(jnp.bfloat16)


def product(state_of, left, right, inner):
    for j in range(2 * NX):
        for group in range(NK // 4):
            terms = right[j][4 * group : 4 * group + 4].reshape(4 * M, M)
            value = lax.dot_general(
                state_of(j), terms, (((1,), (1,)), ((), ())), preferred_element_type=jnp.float32
            ).astype(jnp.bfloat16)
            for n in range(2):
                for part in range(4):
                    k = 4 * group + part
                    inner[n, k * M : (k + 1) * M, j * M : (j + 1) * M] = value[
                        n * M : (n + 1) * M, part * M : (part + 1) * M
                    ]
    for n in range(2):
        row = jnp.concatenate([left[n][k] for k in range(NK)], axis=1)
        yield jnp.dot(row, inner[n], preferred_element_type=jnp.float32)


def products_kernel(tab, *refs):
    left, right, starts = refs[:2], refs[2:10], refs[10:12]
    sent, out0, out1, first, inner = refs[12:]
    x, c, z, y, h = here()

    def states(j):
        return jnp.concatenate([starts[0][j], starts[1][j]], axis=0)

    for n, value in enumerate(product(states, left, right, inner)):
        a = tab[LEFT_ORDER, slot_of(x, c, z + shift_of(tab, y, c, n))]
        for j in range(2 * NX):
            b = right_sector(tab, x, c, z, j)
            block = masked(value[:, j * M : (j + 1) * M], tab, a, b).astype(jnp.bfloat16)
            first[j, n] = block
            to_x, to_c = lax.rem(x + j % NX, NX), c if j < NX else 1 - c
            for to_y in range(NY):
                sent[(to_x * NC + to_c) * NY + to_y, n] = block

    def second_states(j):
        return first[j].reshape(2 * M, M)

    for out, value in zip((out0, out1), product(second_states, left, right, inner)):
        for j in range(2 * NX):
            out[j] = value[:, j * M : (j + 1) * M].astype(jnp.bfloat16)


def first_order_kernel(tab, came, out):
    x, c, z, y, h = here()
    for x_from in range(NX):
        for c_from in range(NC):
            for y_from in range(NY):
                for n in range(2):
                    slot = slot_of(x_from, c_from, z + shift_of(tab, y_from, c_from, n))
                    place = ((x_from * NC + c_from) * NY + y_from) * 2 + n
                    out[tab[LEFT_ORDER, slot]] = came[place]


def second_pack_kernel(tab, back1, back0, *outs):
    x, c, z, y, h = here()
    for out in outs:
        out[...] = jnp.zeros(out.shape, out.dtype)
    for n, back in enumerate((back0, back1)):
        z_from = z - shift_of(tab, y, c, n)
        for j in range(2 * NX):
            b = right_sector(tab, x, c, z_from, j)
            group = b // 8

            for r, out in enumerate(outs):

                @pl.when(group == lax.rem(y + r, NY) * NH + h)
                def _(j=j, b=b, back=back, out=out):
                    out[lax.rem(b, 8)] = back[j]


def second_pick_kernel(tab, part0, part1, part2, part3, out):
    x, c, z, y, h = here()
    a = tab[LEFT_ORDER, slot_of(x, c, z)]
    for q in range(8):
        value = part0[q].astype(jnp.float32)
        for part in (part1, part2, part3):
            value = value + part[q].astype(jnp.float32)
        out[q] = masked(value, tab, a, (y * NH + h) * 8 + q).astype(jnp.bfloat16)


VMEM = pl.BlockSpec(memory_space=pltpu.VMEM)
SMEM = pl.BlockSpec(memory_space=pltpu.SMEM)


def blocks(*shape):
    return jax.ShapeDtypeStruct(shape + (M, M), jnp.bfloat16)


def call(kernel, name, inputs, outputs, scratch=(), flops=0, size=0, vmem=8 << 20):
    return pl.pallas_call(
        kernel,
        name=name,
        out_shape=outputs,
        in_specs=[SMEM if v.dtype == jnp.int32 else VMEM for v in inputs],
        out_specs=jax.tree.map(lambda _: VMEM, outputs),
        scratch_shapes=list(scratch),
        cost_estimate=pl.CostEstimate(flops=flops, bytes_accessed=size, transcendentals=0),
        compiler_params=pltpu.CompilerParams(vmem_limit_bytes=vmem),
    )(*inputs)


def on_device(
    psi, left_ops, right_ops, left_order, right_order, left_qn, right_qn, left_dims, right_dims
):
    h = lax.axis_index("h")
    with jax.named_scope("half_exchange"):
        own = jnp.concatenate([left_ops[:, 0], right_ops[:, 0]], 0)
        other = from_half(own)
    with jax.named_scope("psi_pack"):
        tab = jnp.concatenate(
            [
                jnp.stack([left_order, right_order, left_qn, right_qn, left_dims, right_dims]),
                jnp.asarray(CONSTANT_ROWS),
            ]
        )
        packed = call(psi_kernel, "psi_pack", (tab, psi[0]), [blocks(8)] * 2, size=3 << 20)
    with jax.named_scope("over_y"):
        pieces = [jnp.concatenate([own, other], 0)]
        pieces += [from_y(pieces[0], r) for r in range(1, NY)]
    with jax.named_scope("psi_shift"):
        starts = [from_shift(packed[n], n) for n in range(2)]
    with jax.named_scope("terms"):
        pieces, starts = lax.optimization_barrier((pieces, starts))
        left16, right16 = call(
            terms_kernel, "terms", pieces, [blocks(NK)] * 2, size=2 << 20
        )
    with jax.named_scope("right_core"):
        right_swapped = from_core(right16)
    with jax.named_scope("left_shift"):
        left = [from_shift(left16, n) for n in range(2)]
    with jax.named_scope("right_over_x"):
        right = [right16] + [from_x(right16, r) for r in range(1, NX)]
    with jax.named_scope("right_core"):
        right = right + [right_swapped] + [from_core(value) for value in right[1:]]

    with jax.named_scope("products"):
        sent, *seconds = call(
            products_kernel, "products", (tab, *left, *right, *starts),
            [blocks(NX * NC * NY, 2), blocks(8), blocks(8)],
            [
                pltpu.VMEM((2 * NX, 2, M, M), jnp.bfloat16),
                pltpu.VMEM((2, NK * M, 8 * M), jnp.bfloat16),
            ],
            4 * 16 * NK * 2 * M**3, 8 << 20, 20 << 20,
        )
    with jax.named_scope("first_out"):
        came = lax.all_to_all(sent, ("x", "c", "y"), 0, 0, tiled=True).reshape(64, M, M)
    with jax.named_scope("second_shift"):
        far = to_shift(seconds[1], 1)
        near = to_shift(seconds[0], 0)
    with jax.named_scope("second_over_y"):
        parts = call(
            second_pack_kernel, "second_pack", (tab, far, near), [blocks(8)] * NY, size=2 << 20,
        )
        parts = [parts[0]] + [from_y(parts[r], -r) for r in range(1, NY)]
    with jax.named_scope("first_order"):
        first_out = call(first_order_kernel, "first_order", (tab, came), blocks(64), size=4 << 20)
    first_out, *parts = lax.optimization_barrier((first_out, *parts))
    with jax.named_scope("second_pick"):
        second_out = call(
            second_pick_kernel, "second_pick", (tab, *parts), blocks(8), size=2 << 20
        )
    return first_out[None], second_out[None]


def solution(mesh):
    fine = Mesh(mesh.devices.reshape(NX, NC, NZ, NY, NH), AXES)
    slots, ops = P(SLOT), P(("y", "h"), SLOT)
    return jax.shard_map(
        on_device,
        mesh=fine,
        in_specs=(slots, ops, ops, P(), P(), P(), P(), P(), P()),
        out_specs=(slots, P(SLOT, ("y", "h"))),
        check_vma=False,
    )
```
